512 devices in a mesh: row: 8 (over y_lo, x), col: 8 (over y_hi, core), dep: 8 (over z).
Axes of the slice: x: 4, y: 8 (y_hi: 4, y_lo: 2; y = y_hi * 2 + y_lo), z: 8, core: 2. Of those that a mesh axis runs over, the one named last changes fastest.
Arguments:
- tokens: bfloat16 [512, 12288], P(('col', 'dep'), 'row'), may hold values from -6 to 6
- grad_out: bfloat16 [512, 12288], P(('col', 'dep'), 'row'), may hold values from -6 to 6
- w_in: bfloat16 [12288, 24576], P('row', ('col', 'dep')), may hold values from -0.0546875 to 0.0546875
- w_out: bfloat16 [24576, 12288], P(('col', 'dep'), 'row'), may hold values from -0.0390625 to 0.0390625
Outputs:
- grad_in: bfloat16 [512, 12288], P(('col', 'dep'), 'row')
- grad_w_in: bfloat16 [12288, 24576], P('row', ('col', 'dep'))
- grad_w_out: bfloat16 [24576, 12288], P(('col', 'dep'), 'row')
The draws below stay inside these ranges and needn't reach their ends.
All inputs are finite; a program needn't handle non-finite values.
Results may differ from the reference program's by a relative error of at most 0.005.
Values may be sent and summed in bfloat16 or wider, within the bound.
No kernel may reach another device: no remote copies, remote signals or barrier semaphores. Data moves between devices by JAX's collectives and lax.ppermute only.
A program may use at most 64 MiB of HBM per device.

```python
import math
import jax
import jax.numpy as jnp
from jax import lax

D = 12288
FF = 24576
TOKENS = 512


def block_levels(own_key, dims, pieces, least, top_value):
    def one(axis_at, parts):
        heights = jax.random.uniform(jax.random.fold_in(jax.random.fold_in(own_key, 6), axis_at), (parts,), jnp.float32, least / len(pieces), top_value / len(pieces))
        return jnp.repeat(jnp.exp(heights), dims[axis_at] // parts).reshape((-1,) + (1,) * (len(dims) - axis_at - 1))

    gain = one(*pieces[0])
    for cut in pieces[1:]:
        gain = gain * one(*cut)
    return gain


def gaussian(rng, shape, spread, bound, split=(), kind=jnp.bfloat16):
    result = jax.random.normal(rng, shape, jnp.float32) * spread
    if len(split) > 0:
        result = block_levels(rng, shape, split, -0.22, 0.18) * result
    return jnp.clip(result, min=-bound, max=bound).astype(kind)


def setup_inputs(seed: int = 0) -> dict:
    seeds = jax.random.split(jax.random.key(seed), 5)
    tokens = gaussian(seeds[0], (TOKENS, D), 1.0, 6.0, ((0, 64), (1, 8)))
    grad_out = gaussian(seeds[1], (TOKENS, D), 1.0, 6.0, ((0, 64), (1, 8)))
    w_in = gaussian(seeds[2], (D, FF), D ** -0.5, 0.0546875, ((0, 8), (1, 64)))
    w_out = gaussian(seeds[3], (FF, D), FF ** -0.5, 0.0390625, ((0, 64), (1, 8)))
    return {"tokens": tokens, "grad_out": grad_out, "w_in": w_in, "w_out": w_out}


coef = 0.7978845608

def gelu_value(h):
    u = coef * (h + 0.044715 * h * h * h)
    return 0.5 * h * (1.0 + jnp.tanh(u))

def gelu_slope(h):
    t = jnp.tanh(coef * (h + 0.044715 * h * h * h))
    return 0.5 * (1.0 + t) + 0.5 * h * (1.0 - t * t) * coef * (1.0 + 0.134145 * h * h)

def reference(tokens, grad_out, w_in, w_out):
    pre = jnp.dot(tokens, w_in, preferred_element_type=jnp.float32)
    back = lax.dot_general(grad_out, w_out, (((1,), (1,)), ((), ())), preferred_element_type=jnp.float32)
    act = gelu_value(pre).astype(jnp.bfloat16)
    grad_hidden = (back * gelu_slope(pre)).astype(jnp.bfloat16)
    factor = 1.0 / math.sqrt(TOKENS)
    grad_w_out = lax.dot_general(act, grad_out, (((0,), (0,)), ((), ())), preferred_element_type=jnp.float32)
    grad_w_in = lax.dot_general(tokens, grad_hidden, (((0,), (0,)), ((), ())), preferred_element_type=jnp.float32)
    grad_in = lax.dot_general(grad_hidden, w_in, (((1,), (1,)), ((), ())), preferred_element_type=jnp.float32)
    return (grad_in.astype(jnp.bfloat16), (grad_w_in * factor).astype(jnp.bfloat16), (grad_w_out * factor).astype(jnp.bfloat16))
```

```python
import math

import jax
import jax.numpy as jnp
from jax import lax
from jax.sharding import Mesh, PartitionSpec as P

coef = 0.7978845608
ROWS = ("y_lo", "x")
CHIPS = ("y_hi", "dep")


def gelu_value(h):
    u = coef * (h + 0.044715 * h * h * h)
    return 0.5 * h * (1.0 + jnp.tanh(u))


def gelu_slope(h):
    t = jnp.tanh(coef * (h + 0.044715 * h * h * h))
    return 0.5 * (1.0 + t) + 0.5 * h * (1.0 - t * t) * coef * (1.0 + 0.134145 * h * h)


def dot(a, b, dims):
    return lax.dot_general(a, b, ((dims[:1], dims[1:]), ((), ())), preferred_element_type=jnp.float32)


def spread(block, axes):
    n = lax.axis_size(axes)
    return lax.all_to_all(jnp.broadcast_to(block[None], (n,) + block.shape), axes, 0, 0, tiled=True)


def swap(block):
    return lax.ppermute(block, "core", [(0, 1), (1, 0)])


def shards(tokens, grad_out, w_in, w_out):
    bf16, f32 = jnp.bfloat16, jnp.float32
    width, hidden = w_in.shape
    own = spread(jnp.concatenate([tokens, grad_out], axis=1), CHIPS).reshape(-1, 2 * width)
    half = own.shape[0]
    other = swap(own)

    def partials(block):
        pre = dot(block[:, :width], w_in, (1, 0))
        back = dot(block[:, width:], w_out, (1, 1))
        return jnp.concatenate([pre, back], axis=1).astype(bf16)

    part = jnp.concatenate([partials(own), partials(other)], axis=0)
    n = lax.axis_size(ROWS)
    part = lax.all_to_all(part.reshape(n, -1, 2 * hidden), ROWS, 0, 0, tiled=True)
    total = jnp.sum(part.astype(f32), axis=0)
    pre, back = total[:, :hidden], total[:, hidden:]
    pair = jnp.concatenate([gelu_value(pre).astype(bf16), (back * gelu_slope(pre)).astype(bf16)], axis=1)
    pair = spread(pair, ROWS).reshape(2 * half, 2 * hidden)
    act, grad_hidden = pair[:, :hidden], pair[:, hidden:]

    sent = swap(dot(grad_hidden[half:], w_in, (1, 1)).astype(bf16))
    factor = 1.0 / math.sqrt(2 * half)
    x_all = jnp.concatenate([own[:, :width], other[:, :width]], axis=0)
    dy_all = jnp.concatenate([own[:, width:], other[:, width:]], axis=0)
    grad_w_in = dot(x_all, grad_hidden, (0, 0))
    grad_w_out = dot(act, dy_all, (0, 0))
    input_part = (dot(grad_hidden[:half], w_in, (1, 1)) + sent.astype(f32)).astype(bf16)
    n = lax.axis_size(CHIPS)
    input_part = lax.all_to_all(input_part.reshape(n, -1, width), CHIPS, 0, 0, tiled=True)
    grad_in = jnp.sum(input_part.astype(f32), axis=0)
    return (
        grad_in.astype(bf16),
        (grad_w_in * factor).astype(bf16),
        (grad_w_out * factor).astype(bf16),
    )


def solution(mesh):
    rows, cols, deps = mesh.devices.shape
    fine = Mesh(
        mesh.devices.reshape(2, rows // 2, cols // 2, 2, deps), ("y_lo", "x", "y_hi", "core", "dep")
    )
    blocks = ("y_hi", "core", "dep")
    placed = (P(blocks, ROWS), P(blocks, ROWS), P(ROWS, blocks), P(blocks, ROWS))
    return jax.shard_map(
        shards,
        mesh=fine,
        in_specs=placed,
        out_specs=(P(blocks, ROWS), P(ROWS, blocks), P(blocks, ROWS)),
        check_vma=False,
    )
```

```python
import math

import jax
import jax.numpy as jnp
from jax import lax
from jax.sharding import Mesh, PartitionSpec as P

coef = 0.7978845608
ROWS = ("y_lo", "x")
EVEN = ("z_hi", "y_hi")
CHIPS = ("z_lo",) + EVEN
RING = ("z_hi", "z_lo")


def gelu_value(h):
    u = coef * (h + 0.044715 * h * h * h)
    return 0.5 * h * (1.0 + jnp.tanh(u))


def gelu_slope(h):
    t = jnp.tanh(coef * (h + 0.044715 * h * h * h))
    return 0.5 * (1.0 + t) + 0.5 * h * (1.0 - t * t) * coef * (1.0 + 0.134145 * h * h)


def dot(a, b, dims):
    return lax.dot_general(a, b, ((dims[:1], dims[1:]), ((), ())), preferred_element_type=jnp.float32)


def exchange(blocks, axes):
    return lax.all_to_all(blocks, axes, 0, 0, tiled=True)


def spread(block, axes):
    n = lax.axis_size(axes)
    return exchange(jnp.broadcast_to(block[None], (n,) + block.shape), axes)


def swap(block):
    return lax.ppermute(block, "core", [(0, 1), (1, 0)])


def fetch(block, by):
    n = lax.axis_size(RING)
    return lax.ppermute(block, RING, [((i + by) % n, i) for i in range(n)])


def gather(block):
    near = spread(block, EVEN).reshape(-1, block.shape[1])
    cut = near.shape[0] // 2
    return near, jnp.concatenate([fetch(near[:cut], 1), fetch(near[cut:], -1)], axis=0)


def shards(tokens, grad_out, w_in, w_out):
    bf16, f32 = jnp.bfloat16, jnp.float32
    width, hidden = w_in.shape
    near, far = gather(jnp.concatenate([tokens, grad_out], axis=1))
    w_in, w_out = [w_in, swap(w_in)], [w_out, swap(w_out)]

    def partials(block):
        pre = [dot(block[:, :width], w, (1, 0)).astype(bf16) for w in w_in]
        back = [dot(block[:, width:], w, (1, 1)).astype(bf16) for w in w_out]
        part = jnp.concatenate(pre + back, axis=1)
        return exchange(part.reshape(lax.axis_size(ROWS), -1, 4 * hidden), ROWS)

    part = jnp.concatenate([partials(near), partials(far)], axis=1)
    total = jnp.sum(part.astype(f32), axis=0)
    pre, back = total[:, : 2 * hidden], total[:, 2 * hidden :]
    pair = jnp.concatenate([gelu_value(pre).astype(bf16), (back * gelu_slope(pre)).astype(bf16)], axis=1)
    pair = spread(pair, ROWS).reshape(lax.axis_size(ROWS), 2, -1, 4 * hidden)
    pair = jnp.swapaxes(pair, 0, 1).reshape(-1, 4 * hidden)
    act, grad_hidden = pair[:, : 2 * hidden], pair[:, 2 * hidden :]

    ordered = jnp.where(lax.axis_index("z_lo") == 0, grad_hidden, jnp.roll(grad_hidden, near.shape[0], axis=0))
    input_part = dot(ordered[:, :hidden], w_in[0], (1, 1)) + dot(ordered[:, hidden:], w_in[1], (1, 1))
    input_part = input_part.astype(bf16)
    input_part = exchange(input_part.reshape(lax.axis_size(CHIPS), -1, width), CHIPS)
    grad_in = jnp.sum(input_part.astype(f32), axis=0)

    own = jnp.concatenate([near, far], axis=0)
    other = swap(own)
    act = jnp.concatenate([act[:, :hidden], swap(act[:, hidden:])], axis=0)
    grad_hidden = jnp.concatenate([grad_hidden[:, :hidden], swap(grad_hidden[:, hidden:])], axis=0)
    x_all = jnp.concatenate([own[:, :width], other[:, :width]], axis=0)
    dy_all = jnp.concatenate([own[:, width:], other[:, width:]], axis=0)
    factor = 1.0 / math.sqrt(x_all.shape[0])
    grad_w_in = dot(x_all, grad_hidden, (0, 0))
    grad_w_out = dot(act, dy_all, (0, 0))
    return (
        grad_in.astype(bf16),
        (grad_w_in * factor).astype(bf16),
        (grad_w_out * factor).astype(bf16),
    )


def solution(mesh):
    rows, cols, deps = mesh.devices.shape
    fine = Mesh(
        mesh.devices.reshape(2, rows // 2, cols // 2, 2, deps // 2, 2),
        ("y_lo", "x", "y_hi", "core", "z_hi", "z_lo"),
    )
    blocks = ("y_hi", "core", "z_hi", "z_lo")
    placed = (P(blocks, ROWS), P(blocks, ROWS), P(ROWS, blocks), P(blocks, ROWS))
    return jax.shard_map(
        shards,
        mesh=fine,
        in_specs=placed,
        out_specs=(P(blocks, ROWS), P(ROWS, blocks), P(blocks, ROWS)),
        check_vma=False,
    )
```

```python
import functools
import math

import jax
import jax.numpy as jnp
from jax import lax
from jax.experimental import pallas as pl
from jax.experimental.pallas import tpu as pltpu
from jax.sharding import Mesh, PartitionSpec as P

coef = 0.7978845608
ROWS = ("y_lo", "x")
EVEN = ("z_hi", "y_far", "y_near")
CHIPS = ("z_hi", "y_far", "z_lo", "y_near")
RING = ("z_hi", "z_lo")


def gelu_value(h):
    u = coef * (h + 0.044715 * h * h * h)
    return 0.5 * h * (1.0 + jnp.tanh(u))


def gelu_slope(h):
    t = jnp.tanh(coef * (h + 0.044715 * h * h * h))
    return 0.5 * (1.0 + t) + 0.5 * h * (1.0 - t * t) * coef * (1.0 + 0.134145 * h * h)


def dot(a, b, dims):
    return lax.dot_general(a, b, ((dims[:1], dims[1:]), ((), ())), preferred_element_type=jnp.float32)


def exchange(blocks, axes):
    return lax.all_to_all(blocks, axes, 0, 0, tiled=True)


def spread(block, axes):
    n = lax.axis_size(axes)
    return exchange(jnp.broadcast_to(block[None], (n,) + block.shape), axes)


def swap(block):
    return lax.ppermute(block, "core", [(0, 1), (1, 0)])


def fetch(block, by):
    n = lax.axis_size(RING)
    return lax.ppermute(block, RING, [((i + by) % n, i) for i in range(n)])


def gather(block):
    near = spread(block, EVEN).reshape(-1, block.shape[1])
    cut = near.shape[0] // 2
    return near, [fetch(near[:cut], 1), fetch(near[cut:], -1)]


def load(weights, held, arrived):
    copies = [pltpu.make_async_copy(w, h, arrived.at[i]) for i, (w, h) in enumerate(zip(weights, held))]
    for copy in copies:
        copy.start()
    return copies


def with_weights(kernel, out_shape, blocks, weights, cost):
    vmem = pl.BlockSpec(memory_space=pltpu.VMEM)
    cut = len(weights) // 2
    others = [pltpu.with_memory_space_constraint(w, pltpu.HBM) for w in weights[cut:]]
    return pl.pallas_call(
        kernel,
        out_shape=out_shape,
        in_specs=[vmem] * len(blocks)
        + [pl.BlockSpec(memory_space=pl.ANY)] * cut
        + [pl.BlockSpec(memory_space=pltpu.HBM)] * len(others),
        out_specs=vmem,
        scratch_shapes=[pltpu.VMEM(w.shape, w.dtype) for w in weights]
        + [pltpu.SemaphoreType.DMA((len(weights),))],
        compiler_params=pltpu.CompilerParams(vmem_limit_bytes=16 * 2**20),
        cost_estimate=cost,
    )(*blocks, *weights[:cut], *others)


def products_kernel(count, *refs):
    blocks, weights, out = refs[:count], refs[count : count + 4], refs[count + 4]
    held, arrived = refs[count + 5 : count + 9], refs[count + 9]
    copies = load(weights, held, arrived)
    block = jnp.concatenate([b[...] for b in blocks], axis=0)
    width, hidden = held[0].shape
    for i, place in enumerate((0, 2, 1, 3)):
        copies[i].wait()
        if place < 2:
            part = dot(block[:, :width], held[i][...], (1, 0))
        else:
            part = dot(block[:, width:], held[i][...], (1, 1))
        out[:, place * hidden : (place + 1) * hidden] = part.astype(out.dtype)


def products(blocks, w_in, w_out, weight):
    rows, (width, hidden) = sum(b.shape[0] for b in blocks), w_in[0].shape
    return with_weights(
        functools.partial(products_kernel, len(blocks)),
        jax.ShapeDtypeStruct((rows, 4 * hidden), jnp.bfloat16),
        blocks,
        [w_in[0], w_out[0], w_in[1], w_out[1]],
        pl.CostEstimate(
            flops=8 * weight * rows * width * hidden, bytes_accessed=8 * width * hidden, transcendentals=0
        ),
    )


def input_kernel(pair, w_mine, w_other, out, mine, other, arrived):
    copies = load((w_mine, w_other), (mine, other), arrived)
    hidden = mine.shape[1]
    copies[0].wait()
    total = dot(pair[:, 2 * hidden : 3 * hidden], mine[...], (1, 1))
    copies[1].wait()
    out[...] = (total + dot(pair[:, 3 * hidden :], other[...], (1, 1))).astype(out.dtype)


def input_products(pair, w_in):
    rows, (width, hidden) = pair.shape[0], w_in[0].shape
    return with_weights(
        input_kernel,
        jax.ShapeDtypeStruct((rows, width), jnp.bfloat16),
        [pair],
        w_in,
        pl.CostEstimate(
            flops=4 * rows * width * hidden, bytes_accessed=6 * width * hidden, transcendentals=0
        ),
    )


def shards(tokens, grad_out, w_in, w_out):
    bf16, f32 = jnp.bfloat16, jnp.float32
    width, hidden = w_in.shape
    rows = lax.axis_size(ROWS)
    low = lax.axis_index("z_lo") == 0

    def by_z(near, far):
        both = jnp.where(low, near, far), jnp.where(low, far, near)
        return jnp.concatenate(both, axis=-2)

    near, far = gather(jnp.concatenate([tokens, grad_out], axis=1))
    w_in, w_out = [w_in, swap(w_in)], [w_out, swap(w_out)]
    parts = products([near], w_in, w_out, 1), products(far, w_in, w_out, 25)
    parts = [exchange(part.reshape(rows, -1, 4 * hidden), ROWS) for part in parts]
    total = by_z(*[jnp.sum(part.astype(f32), axis=0) for part in parts])
    pre, back = total[:, : 2 * hidden], total[:, 2 * hidden :]
    pair = jnp.concatenate([gelu_value(pre).astype(bf16), (back * gelu_slope(pre)).astype(bf16)], axis=1)
    pair = spread(pair, ROWS).reshape(-1, 4 * hidden)
    act, grad_hidden = pair[:, : 2 * hidden], pair[:, 2 * hidden :]

    input_part = exchange(input_products(pair, w_in).reshape(lax.axis_size(CHIPS), -1, width), CHIPS)
    grad_in = jnp.sum(input_part.astype(f32), axis=0)

    far = jnp.concatenate(far, axis=0)
    own = by_z(*[block.reshape(rows, -1, 2 * width) for block in (near, far)]).reshape(-1, 2 * width)
    other = swap(own)
    act = jnp.concatenate([act[:, :hidden], swap(act[:, hidden:])], axis=0)
    grad_hidden = jnp.concatenate([grad_hidden[:, :hidden], swap(grad_hidden[:, hidden:])], axis=0)
    x_all = jnp.concatenate([own[:, :width], other[:, :width]], axis=0)
    dy_all = jnp.concatenate([own[:, width:], other[:, width:]], axis=0)
    factor = 1.0 / math.sqrt(x_all.shape[0])
    grad_w_in = dot(x_all, grad_hidden, (0, 0))
    grad_w_out = dot(act, dy_all, (0, 0))
    return (
        grad_in.astype(bf16),
        (grad_w_in * factor).astype(bf16),
        (grad_w_out * factor).astype(bf16),
    )


def solution(mesh):
    rows, cols, deps = mesh.devices.shape
    fine = Mesh(
        mesh.devices.reshape(2, rows // 2, cols // 4, 2, 2, deps // 2, 2),
        ("y_lo", "x", "y_far", "y_near", "core", "z_hi", "z_lo"),
    )
    blocks = ("y_far", "y_near", "core", "z_hi", "z_lo")
    placed = (P(blocks, ROWS), P(blocks, ROWS), P(ROWS, blocks), P(blocks, ROWS))
    return jax.shard_map(
        shards,
        mesh=fine,
        in_specs=placed,
        out_specs=(P(blocks, ROWS), P(ROWS, blocks), P(blocks, ROWS)),
        check_vma=False,
    )
```

```python
import functools
import math

import jax
import jax.numpy as jnp
from jax import lax
from jax.experimental import pallas as pl
from jax.experimental.pallas import tpu as pltpu
from jax.sharding import Mesh, PartitionSpec as P

coef = 0.7978845608
ROWS = ("y_lo", "x")
EVEN = ("y_near", "y_far", "z_hi", "z_mid")
CHIPS = ("y_near", "y_far", "z_hi", "z_lo", "z_mid")
RING = ("z_hi", "z_mid", "z_lo")


def gelu_value(h):
    u = coef * (h + 0.044715 * h * h * h)
    return 0.5 * h * (1.0 + jnp.tanh(u))


def gelu_slope(h):
    t = jnp.tanh(coef * (h + 0.044715 * h * h * h))
    return 0.5 * (1.0 + t) + 0.5 * h * (1.0 - t * t) * coef * (1.0 + 0.134145 * h * h)


def dot(a, b, dims):
    return lax.dot_general(a, b, ((dims[:1], dims[1:]), ((), ())), preferred_element_type=jnp.float32)


def exchange(blocks, axes):
    return lax.all_to_all(blocks, axes, 0, 0, tiled=True)


def spread(block, axes):
    n = lax.axis_size(axes)
    return exchange(jnp.broadcast_to(block[None], (n,) + block.shape), axes)


def swap(block):
    return lax.ppermute(block, "core", [(0, 1), (1, 0)])


def fetch(block, by):
    n = lax.axis_size(RING)
    return lax.ppermute(block, RING, [((i + by) % n, i) for i in range(n)])


def gather(block):
    near = spread(block, EVEN).reshape(-1, block.shape[1])
    cut = near.shape[0] // 2
    return near, [fetch(near[:cut], 1), fetch(near[cut:], -1)]


VMEM = pl.BlockSpec(memory_space=pltpu.VMEM)
HBM = pl.BlockSpec(memory_space=pltpu.HBM)
PARAMS = pltpu.CompilerParams(vmem_limit_bytes=16 * 2**20)


def in_hbm(*arrays):
    return [pltpu.with_memory_space_constraint(a, pltpu.HBM) for a in arrays]


def start_all(places, arrived):
    copies = [pltpu.make_async_copy(a, b, arrived.at[i]) for i, (a, b) in enumerate(places)]
    for copy in copies:
        copy.start()
    return copies


def hold_kernel(w_in, w_out, held_in, held_out, arrived):
    for copy in start_all([(w_in, held_in), (w_out, held_out)], arrived):
        copy.wait()


def hold(w_in, w_out):
    return pl.pallas_call(
        hold_kernel,
        out_shape=(pltpu.VMEM(w_in.shape, w_in.dtype), pltpu.VMEM(w_out.shape, w_out.dtype)),
        in_specs=[HBM, HBM],
        out_specs=(VMEM, VMEM),
        scratch_shapes=[pltpu.SemaphoreType.DMA((2,))],
        compiler_params=PARAMS,
        cost_estimate=pl.CostEstimate(flops=0, bytes_accessed=8 * w_in.size, transcendentals=0),
    )(*in_hbm(w_in, w_out))


def products_kernel(count, *refs):
    blocks = refs[:count]
    w_in, w_out, w_in_other, w_out_other, part, block, in_held, out_held, total, arrived, sent = refs[count:]
    width, hidden = w_in.shape
    rows = blocks[0].shape[0]
    copies = start_all(
        [(b, block.at[pl.ds(i * rows, rows)]) for i, b in enumerate(blocks)]
        + [(w_in_other, in_held), (w_out_other, out_held)],
        arrived,
    )
    for copy in copies[:count]:
        copy.wait()
    results = []
    for i, weight in enumerate((w_in, w_out, in_held, out_held)):
        if i >= 2:
            copies[count + i - 2].wait()
        if i % 2 == 0:
            value = dot(block[:, :width], weight[...], (1, 0))
        else:
            value = dot(block[:, width:], weight[...], (1, 1))
        place = pl.ds((i // 2 + 2 * (i % 2)) * hidden, hidden)
        total[:, place] = value.astype(total.dtype)
        results.append(pltpu.make_async_copy(total.at[:, place], part.at[:, place], sent.at[i]))
        results[i].start()
    for result in results:
        result.wait()


def products(blocks, held, others, weight):
    rows, (width, hidden) = sum(b.shape[0] for b in blocks), held[0].shape
    dtype, count = blocks[0].dtype, len(blocks)
    return pl.pallas_call(
        functools.partial(products_kernel, count),
        out_shape=jax.ShapeDtypeStruct((rows, 4 * hidden), dtype),
        in_specs=[pl.BlockSpec(memory_space=pl.ANY)] * count + [VMEM] * 2 + [HBM] * 2,
        out_specs=HBM,
        scratch_shapes=[
            pltpu.VMEM((rows, 2 * width), dtype),
            pltpu.VMEM((width, hidden), dtype),
            pltpu.VMEM((hidden, width), dtype),
            pltpu.VMEM((rows, 4 * hidden), dtype),
            pltpu.SemaphoreType.DMA((count + 2,)),
            pltpu.SemaphoreType.DMA((4,)),
        ],
        compiler_params=PARAMS,
        cost_estimate=pl.CostEstimate(
            flops=8 * weight * rows * width * hidden, bytes_accessed=8 * width * hidden, transcendentals=0
        ),
    )(*blocks, *held, *in_hbm(*others))


def input_kernel(pair, w_mine, w_other, out, grad_hidden, mine, other, total, arrived, sent):
    width, hidden = mine.shape
    cut = width // 3
    pieces = [pl.ds(i * cut, cut) for i in range(3)]
    places = [(pair.at[:, 2 * hidden :], grad_hidden)]
    for piece in pieces:
        places += [(w_mine.at[piece], mine.at[piece]), (w_other.at[piece], other.at[piece])]
    copies = start_all(places, arrived)
    copies[0].wait()
    results = []
    for i, piece in enumerate(pieces):
        copies[1 + 2 * i].wait()
        value = dot(grad_hidden[:, :hidden], mine[piece, :], (1, 1))
        copies[2 + 2 * i].wait()
        value = value + dot(grad_hidden[:, hidden:], other[piece, :], (1, 1))
        total[:, piece] = value.astype(total.dtype)
        results.append(pltpu.make_async_copy(total.at[:, piece], out.at[:, piece], sent.at[i]))
        results[i].start()
    for result in results:
        result.wait()


def input_products(pair, w_in):
    rows, (width, hidden) = pair.shape[0], w_in[0].shape
    return pl.pallas_call(
        input_kernel,
        out_shape=jax.ShapeDtypeStruct((rows, width), pair.dtype),
        in_specs=[pl.BlockSpec(memory_space=pl.ANY)] + [HBM] * 2,
        out_specs=HBM,
        scratch_shapes=[
            pltpu.VMEM((rows, 2 * hidden), pair.dtype),
            pltpu.VMEM((width, hidden), pair.dtype),
            pltpu.VMEM((width, hidden), pair.dtype),
            pltpu.VMEM((rows, width), pair.dtype),
            pltpu.SemaphoreType.DMA((7,)),
            pltpu.SemaphoreType.DMA((3,)),
        ],
        compiler_params=PARAMS,
        cost_estimate=pl.CostEstimate(
            flops=4 * rows * width * hidden, bytes_accessed=6 * width * hidden, transcendentals=0
        ),
    )(pair, *in_hbm(*w_in))


def shards(tokens, grad_out, w_in, w_out):
    bf16, f32 = jnp.bfloat16, jnp.float32
    width, hidden = w_in.shape
    rows = lax.axis_size(ROWS)

    low = lax.axis_index("z_lo") == 0

    def by_z(near, far):
        return jnp.concatenate([jnp.where(low, near, far), jnp.where(low, far, near)], axis=-2)

    near, far = gather(jnp.concatenate([tokens, grad_out], axis=1))
    held, others = hold(w_in, w_out), [swap(w_in), swap(w_out)]
    parts = products([near], held, others, 25), products(far, held, others, 25)
    parts = [exchange(part.reshape(rows, -1, 4 * hidden), ROWS) for part in parts]
    total = by_z(*[jnp.sum(part.astype(f32), axis=0) for part in parts])
    pre, back = total[:, : 2 * hidden], total[:, 2 * hidden :]
    pair = jnp.concatenate([gelu_value(pre).astype(bf16), (back * gelu_slope(pre)).astype(bf16)], axis=1)
    pair = spread(pair, ROWS).reshape(-1, 4 * hidden)
    input_part = exchange(input_products(pair, [w_in, others[0]]).reshape(lax.axis_size(CHIPS), -1, width), CHIPS)
    grad_in = jnp.sum(input_part.astype(f32), axis=0)

    act, grad_hidden = pair[:, : 2 * hidden], pair[:, 2 * hidden :]
    far = jnp.concatenate(far, axis=0)
    own = by_z(*[b.reshape(rows, -1, 2 * width) for b in (near, far)]).reshape(-1, 2 * width)
    other = swap(own)
    act = jnp.concatenate([act[:, :hidden], swap(act[:, hidden:])], axis=0)
    grad_hidden = jnp.concatenate([grad_hidden[:, :hidden], swap(grad_hidden[:, hidden:])], axis=0)
    x_all = jnp.concatenate([own[:, :width], other[:, :width]], axis=0)
    dy_all = jnp.concatenate([own[:, width:], other[:, width:]], axis=0)
    factor = 1.0 / math.sqrt(x_all.shape[0])
    grad_w_in = dot(x_all, grad_hidden, (0, 0))
    grad_w_out = dot(act, dy_all, (0, 0))
    return (
        grad_in.astype(bf16),
        (grad_w_in * factor).astype(bf16),
        (grad_w_out * factor).astype(bf16),
    )


def solution(mesh):
    rows, cols, deps = mesh.devices.shape
    fine = Mesh(
        mesh.devices.reshape(2, rows // 2, cols // 4, 2, 2, 2, deps // 4, 2),
        ("y_lo", "x", "y_far", "y_near", "core", "z_hi", "z_mid", "z_lo"),
    )
    blocks = ("y_far", "y_near", "core", "z_hi", "z_mid", "z_lo")
    placed = (P(blocks, ROWS), P(blocks, ROWS), P(ROWS, blocks), P(blocks, ROWS))
    return jax.shard_map(
        shards,
        mesh=fine,
        in_specs=placed,
        out_specs=(P(blocks, ROWS), P(ROWS, blocks), P(blocks, ROWS)),
        check_vma=False,
    )
```

```python
import functools
import math

import jax
import jax.numpy as jnp
from jax import lax
from jax.experimental import pallas as pl
from jax.experimental.pallas import tpu as pltpu
from jax.sharding import Mesh, PartitionSpec as P

coef = 0.7978845608
ROWS = ("y_lo", "x")
EVEN = ("y_far", "y_near", "z_hi", "z_mid")
CHIPS = ("y_far", "y_near", "z_hi", "z_lo", "z_mid")
RING = ("z_hi", "z_mid", "z_lo")


def gelu_value(h):
    u = coef * (h + 0.044715 * h * h * h)
    return 0.5 * h * (1.0 + jnp.tanh(u))


def gelu_slope(h):
    t = jnp.tanh(coef * (h + 0.044715 * h * h * h))
    return 0.5 * (1.0 + t) + 0.5 * h * (1.0 - t * t) * coef * (1.0 + 0.134145 * h * h)


def dot(a, b, dims):
    return lax.dot_general(a, b, ((dims[:1], dims[1:]), ((), ())), preferred_element_type=jnp.float32)


def exchange(blocks, axes):
    return lax.all_to_all(blocks, axes, 0, 0, tiled=True)


def spread(block, axes):
    n = lax.axis_size(axes)
    return exchange(jnp.broadcast_to(block[None], (n,) + block.shape), axes)


def swap(block):
    return lax.ppermute(block, "core", [(0, 1), (1, 0)])


def fetch(block, by):
    n = lax.axis_size(RING)
    return lax.ppermute(block, RING, [((i + by) % n, i) for i in range(n)])


def gather(block):
    near = spread(block, EVEN).reshape(-1, block.shape[1])
    cut = near.shape[0] // 2
    return near, [fetch(near[:cut], 1), fetch(near[cut:], -1)]


VMEM = pl.BlockSpec(memory_space=pltpu.VMEM)
HBM = pl.BlockSpec(memory_space=pltpu.HBM)
PARAMS = pltpu.CompilerParams(vmem_limit_bytes=16 * 2**20)


def in_hbm(*arrays):
    return [pltpu.with_memory_space_constraint(a, pltpu.HBM) for a in arrays]


def start_all(places, arrived):
    copies = [pltpu.make_async_copy(a, b, arrived.at[i]) for i, (a, b) in enumerate(places)]
    for copy in copies:
        copy.start()
    return copies


def hold_kernel(w_in, w_out, held_in, held_out, arrived):
    for copy in start_all([(w_in, held_in), (w_out, held_out)], arrived):
        copy.wait()


def hold(w_in, w_out):
    return pl.pallas_call(
        hold_kernel,
        out_shape=(pltpu.VMEM(w_in.shape, w_in.dtype), pltpu.VMEM(w_out.shape, w_out.dtype)),
        in_specs=[HBM, HBM],
        out_specs=(VMEM, VMEM),
        scratch_shapes=[pltpu.SemaphoreType.DMA((2,))],
        compiler_params=PARAMS,
        cost_estimate=pl.CostEstimate(flops=0, bytes_accessed=8 * w_in.size, transcendentals=0),
    )(*in_hbm(w_in, w_out))


def products_kernel(count, *refs):
    blocks = refs[:count]
    w_in, w_out, w_in_other, w_out_other, part, block, in_held, out_held, total, arrived, sent = refs[count:]
    width, hidden = w_in.shape
    rows = blocks[0].shape[0]
    copies = start_all(
        [(b, block.at[pl.ds(i * rows, rows)]) for i, b in enumerate(blocks)]
        + [(w_in_other, in_held), (w_out_other, out_held)],
        arrived,
    )
    for copy in copies[:count]:
        copy.wait()
    results = []
    for i, weight in enumerate((w_in, w_out, in_held, out_held)):
        if i >= 2:
            copies[count + i - 2].wait()
        if i % 2 == 0:
            value = dot(block[:, :width], weight[...], (1, 0))
        else:
            value = dot(block[:, width:], weight[...], (1, 1))
        place = pl.ds((i // 2 + 2 * (i % 2)) * hidden, hidden)
        total[:, place] = value.astype(total.dtype)
        results.append(pltpu.make_async_copy(total.at[:, place], part.at[:, place], sent.at[i]))
        results[i].start()
    for result in results:
        result.wait()


def products(blocks, held, others, weight):
    rows, (width, hidden) = sum(b.shape[0] for b in blocks), held[0].shape
    dtype, count = blocks[0].dtype, len(blocks)
    return pl.pallas_call(
        functools.partial(products_kernel, count),
        out_shape=jax.ShapeDtypeStruct((rows, 4 * hidden), dtype),
        in_specs=[pl.BlockSpec(memory_space=pl.ANY)] * count + [VMEM] * 2 + [HBM] * 2,
        out_specs=HBM,
        scratch_shapes=[
            pltpu.VMEM((rows, 2 * width), dtype),
            pltpu.VMEM((width, hidden), dtype),
            pltpu.VMEM((hidden, width), dtype),
            pltpu.VMEM((rows, 4 * hidden), dtype),
            pltpu.SemaphoreType.DMA((count + 2,)),
            pltpu.SemaphoreType.DMA((4,)),
        ],
        compiler_params=PARAMS,
        cost_estimate=pl.CostEstimate(
            flops=8 * weight * rows * width * hidden, bytes_accessed=8 * width * hidden, transcendentals=0
        ),
    )(*blocks, *held, *in_hbm(*others))


def input_kernel(pair, w_mine, w_other, out, grad_hidden, mine, other, total, arrived, sent):
    width, hidden = mine.shape
    cut = width // 3
    pieces = [pl.ds(i * cut, cut) for i in range(3)]
    places = [(pair.at[:, 2 * hidden :], grad_hidden)]
    for piece in pieces:
        places += [(w_mine.at[piece], mine.at[piece]), (w_other.at[piece], other.at[piece])]
    copies = start_all(places, arrived)
    copies[0].wait()
    results = []
    for i, piece in enumerate(pieces):
        copies[1 + 2 * i].wait()
        value = dot(grad_hidden[:, :hidden], mine[piece, :], (1, 1))
        copies[2 + 2 * i].wait()
        value = value + dot(grad_hidden[:, hidden:], other[piece, :], (1, 1))
        total[:, piece] = value.astype(total.dtype)
        results.append(pltpu.make_async_copy(total.at[:, piece], out.at[:, piece], sent.at[i]))
        results[i].start()
    for result in results:
        result.wait()


def input_products(pair, w_in):
    rows, (width, hidden) = pair.shape[0], w_in[0].shape
    return pl.pallas_call(
        input_kernel,
        out_shape=jax.ShapeDtypeStruct((rows, width), pair.dtype),
        in_specs=[pl.BlockSpec(memory_space=pl.ANY)] + [HBM] * 2,
        out_specs=HBM,
        scratch_shapes=[
            pltpu.VMEM((rows, 2 * hidden), pair.dtype),
            pltpu.VMEM((width, hidden), pair.dtype),
            pltpu.VMEM((width, hidden), pair.dtype),
            pltpu.VMEM((rows, width), pair.dtype),
            pltpu.SemaphoreType.DMA((7,)),
            pltpu.SemaphoreType.DMA((3,)),
        ],
        compiler_params=PARAMS,
        cost_estimate=pl.CostEstimate(
            flops=4 * rows * width * hidden, bytes_accessed=6 * width * hidden, transcendentals=0
        ),
    )(pair, *in_hbm(*w_in))


def shards(tokens, grad_out, w_in, w_out):
    bf16, f32 = jnp.bfloat16, jnp.float32
    width, hidden = w_in.shape
    rows = lax.axis_size(ROWS)

    low = lax.axis_index("z_lo") == 0

    def by_z(near, far):
        return jnp.concatenate([jnp.where(low, near, far), jnp.where(low, far, near)], axis=-2)

    near, far = gather(jnp.concatenate([tokens, grad_out], axis=1))
    held, others = hold(w_in, w_out), [swap(w_in), swap(w_out)]
    parts = products([near], held, others, 25), products(far, held, others, 25)
    parts = [exchange(part.reshape(rows, -1, 4 * hidden), ROWS) for part in parts]
    total = by_z(*[jnp.sum(part.astype(f32), axis=0) for part in parts])
    pre, back = total[:, : 2 * hidden], total[:, 2 * hidden :]
    pair = jnp.concatenate([gelu_value(pre).astype(bf16), (back * gelu_slope(pre)).astype(bf16)], axis=1)
    pair = spread(pair, ROWS).reshape(-1, 4 * hidden)
    input_part = exchange(input_products(pair, [w_in, others[0]]).reshape(lax.axis_size(CHIPS), -1, width), CHIPS)
    grad_in = jnp.sum(input_part.astype(f32), axis=0)

    act, grad_hidden = pair[:, : 2 * hidden], pair[:, 2 * hidden :]
    far = jnp.concatenate(far, axis=0)
    own = by_z(*[b.reshape(rows, -1, 2 * width) for b in (near, far)]).reshape(-1, 2 * width)
    other = swap(own)
    act = jnp.concatenate([act[:, :hidden], swap(act[:, hidden:])], axis=0)
    grad_hidden = jnp.concatenate([grad_hidden[:, :hidden], swap(grad_hidden[:, hidden:])], axis=0)
    x_all = jnp.concatenate([own[:, :width], other[:, :width]], axis=0)
    dy_all = jnp.concatenate([own[:, width:], other[:, width:]], axis=0)
    factor = 1.0 / math.sqrt(x_all.shape[0])
    grad_w_in = dot(x_all, grad_hidden, (0, 0))
    grad_w_out = dot(act, dy_all, (0, 0))
    return (
        grad_in.astype(bf16),
        (grad_w_in * factor).astype(bf16),
        (grad_w_out * factor).astype(bf16),
    )


def solution(mesh):
    rows, cols, deps = mesh.devices.shape
    fine = Mesh(
        mesh.devices.reshape(2, rows // 2, cols // 4, 2, 2, 2, deps // 4, 2),
        ("y_lo", "x", "y_far", "y_near", "core", "z_hi", "z_mid", "z_lo"),
    )
    blocks = ("y_far", "y_near", "core", "z_hi", "z_mid", "z_lo")
    placed = (P(blocks, ROWS), P(blocks, ROWS), P(ROWS, blocks), P(blocks, ROWS))
    return jax.shard_map(
        shards,
        mesh=fine,
        in_specs=placed,
        out_specs=(P(blocks, ROWS), P(ROWS, blocks), P(blocks, ROWS)),
        check_vma=False,
    )
```

```python
import functools
import math

import jax
import jax.numpy as jnp
from jax import lax
from jax.experimental import pallas as pl
from jax.experimental.pallas import tpu as pltpu
from jax.sharding import Mesh, PartitionSpec as P

coef = 0.7978845608
ROWS = ("y_lo", "x")
EVEN = ("y_far", "y_near", "z_hi", "z_mid")
CHIPS = ("y_far", "y_near", "z_hi", "z_lo", "z_mid")
RING = ("z_hi", "z_mid", "z_lo")


def gelu_value(h):
    u = coef * (h + 0.044715 * h * h * h)
    return 0.5 * h * (1.0 + jnp.tanh(u))


def gelu_slope(h):
    t = jnp.tanh(coef * (h + 0.044715 * h * h * h))
    return 0.5 * (1.0 + t) + 0.5 * h * (1.0 - t * t) * coef * (1.0 + 0.134145 * h * h)


def dot(a, b, dims):
    return lax.dot_general(a, b, ((dims[:1], dims[1:]), ((), ())), preferred_element_type=jnp.float32)


def exchange(blocks, axes):
    return lax.all_to_all(blocks, axes, 0, 0, tiled=True)


def spread(block, axes):
    n = lax.axis_size(axes)
    return exchange(jnp.broadcast_to(block[None], (n,) + block.shape), axes)


def swap(block):
    return lax.ppermute(block, "core", [(0, 1), (1, 0)])


def fetch(block, by):
    n = lax.axis_size(RING)
    return lax.ppermute(block, RING, [((i + by) % n, i) for i in range(n)])


def gather(block):
    near = spread(block, EVEN).reshape(-1, block.shape[1])
    cut = near.shape[0] // 2
    return near, [fetch(near[:cut], 1), fetch(near[cut:], -1)]


VMEM = pl.BlockSpec(memory_space=pltpu.VMEM)
HBM = pl.BlockSpec(memory_space=pltpu.HBM)
PARAMS = pltpu.CompilerParams(vmem_limit_bytes=16 * 2**20)


def in_hbm(*arrays):
    return [pltpu.with_memory_space_constraint(a, pltpu.HBM) for a in arrays]


def start_all(places, arrived):
    copies = [pltpu.make_async_copy(a, b, arrived.at[i]) for i, (a, b) in enumerate(places)]
    for copy in copies:
        copy.start()
    return copies


def hold_kernel(w_in, w_out, held_in, held_out, arrived):
    for copy in start_all([(w_in, held_in), (w_out, held_out)], arrived):
        copy.wait()


def hold(w_in, w_out):
    return pl.pallas_call(
        hold_kernel,
        out_shape=(pltpu.VMEM(w_in.shape, w_in.dtype), pltpu.VMEM(w_out.shape, w_out.dtype)),
        in_specs=[HBM, HBM],
        out_specs=(VMEM, VMEM),
        scratch_shapes=[pltpu.SemaphoreType.DMA((2,))],
        compiler_params=PARAMS,
        cost_estimate=pl.CostEstimate(flops=0, bytes_accessed=8 * w_in.size, transcendentals=0),
    )(*in_hbm(w_in, w_out))


def products_kernel(count, *refs):
    blocks = refs[:count]
    w_in, w_out, w_in_other, w_out_other, part, block, in_held, out_held, total, arrived, sent = refs[count:]
    width, hidden = w_in.shape
    rows = blocks[0].shape[0]
    copies = start_all(
        [(b, block.at[pl.ds(i * rows, rows)]) for i, b in enumerate(blocks)]
        + [(w_in_other, in_held), (w_out_other, out_held)],
        arrived,
    )
    for copy in copies[:count]:
        copy.wait()
    results = []
    for i, weight in enumerate((w_in, w_out, in_held, out_held)):
        if i >= 2:
            copies[count + i - 2].wait()
        if i % 2 == 0:
            value = dot(block[:, :width], weight[...], (1, 0))
        else:
            value = dot(block[:, width:], weight[...], (1, 1))
        place = pl.ds((i // 2 + 2 * (i % 2)) * hidden, hidden)
        total[:, place] = value.astype(total.dtype)
        results.append(pltpu.make_async_copy(total.at[:, place], part.at[:, place], sent.at[i]))
        results[i].start()
    for result in results:
        result.wait()


def products(blocks, held, others, weight):
    rows, (width, hidden) = sum(b.shape[0] for b in blocks), held[0].shape
    dtype, count = blocks[0].dtype, len(blocks)
    return pl.pallas_call(
        functools.partial(products_kernel, count),
        out_shape=jax.ShapeDtypeStruct((rows, 4 * hidden), dtype),
        in_specs=[HBM] * count + [VMEM] * 2 + [HBM] * 2,
        out_specs=HBM,
        scratch_shapes=[
            pltpu.VMEM((rows, 2 * width), dtype),
            pltpu.VMEM((width, hidden), dtype),
            pltpu.VMEM((hidden, width), dtype),
            pltpu.VMEM((rows, 4 * hidden), dtype),
            pltpu.SemaphoreType.DMA((count + 2,)),
            pltpu.SemaphoreType.DMA((4,)),
        ],
        compiler_params=PARAMS,
        cost_estimate=pl.CostEstimate(
            flops=8 * weight * rows * width * hidden, bytes_accessed=8 * width * hidden, transcendentals=0
        ),
    )(*in_hbm(*blocks), *held, *in_hbm(*others))


def input_kernel(pair, w_mine, w_other, out, grad_hidden, mine, other, total, arrived, sent):
    width, hidden = mine.shape
    cut = width // 3
    pieces = [pl.ds(i * cut, cut) for i in range(3)]
    places = [(pair.at[:, 2 * hidden :], grad_hidden)]
    for piece in pieces:
        places += [(w_mine.at[piece], mine.at[piece]), (w_other.at[piece], other.at[piece])]
    copies = start_all(places, arrived)
    copies[0].wait()
    results = []
    for i, piece in enumerate(pieces):
        copies[1 + 2 * i].wait()
        value = dot(grad_hidden[:, :hidden], mine[piece, :], (1, 1))
        copies[2 + 2 * i].wait()
        value = value + dot(grad_hidden[:, hidden:], other[piece, :], (1, 1))
        total[:, piece] = value.astype(total.dtype)
        results.append(pltpu.make_async_copy(total.at[:, piece], out.at[:, piece], sent.at[i]))
        results[i].start()
    for result in results:
        result.wait()


def input_products(pair, w_in):
    rows, (width, hidden) = pair.shape[0], w_in[0].shape
    return pl.pallas_call(
        input_kernel,
        out_shape=jax.ShapeDtypeStruct((rows, width), pair.dtype),
        in_specs=[pl.BlockSpec(memory_space=pl.ANY)] + [HBM] * 2,
        out_specs=HBM,
        scratch_shapes=[
            pltpu.VMEM((rows, 2 * hidden), pair.dtype),
            pltpu.VMEM((width, hidden), pair.dtype),
            pltpu.VMEM((width, hidden), pair.dtype),
            pltpu.VMEM((rows, width), pair.dtype),
            pltpu.SemaphoreType.DMA((7,)),
            pltpu.SemaphoreType.DMA((3,)),
        ],
        compiler_params=PARAMS,
        cost_estimate=pl.CostEstimate(
            flops=4 * rows * width * hidden, bytes_accessed=6 * width * hidden, transcendentals=0
        ),
    )(pair, *in_hbm(*w_in))


def shards(tokens, grad_out, w_in, w_out):
    bf16, f32 = jnp.bfloat16, jnp.float32
    width, hidden = w_in.shape
    rows = lax.axis_size(ROWS)

    low = lax.axis_index("z_lo") == 0

    def by_z(near, far):
        return jnp.concatenate([jnp.where(low, near, far), jnp.where(low, far, near)], axis=-2)

    near, far = gather(jnp.concatenate([tokens, grad_out], axis=1))
    held, others = hold(w_in, w_out), [swap(w_in), swap(w_out)]
    parts = products([near], held, others, 25), products(far, held, others, 25)
    parts = [exchange(part.reshape(rows, -1, 4 * hidden), ROWS) for part in parts]
    total = by_z(*[jnp.sum(part.astype(f32), axis=0) for part in parts])
    pre, back = total[:, : 2 * hidden], total[:, 2 * hidden :]
    pair = jnp.concatenate([gelu_value(pre).astype(bf16), (back * gelu_slope(pre)).astype(bf16)], axis=1)
    pair = spread(pair, ROWS).reshape(-1, 4 * hidden)
    input_part = exchange(input_products(pair, [w_in, others[0]]).reshape(lax.axis_size(CHIPS), -1, width), CHIPS)
    grad_in = jnp.sum(input_part.astype(f32), axis=0)

    act, grad_hidden = pair[:, : 2 * hidden], pair[:, 2 * hidden :]
    far = jnp.concatenate(far, axis=0)
    own = by_z(*[b.reshape(rows, -1, 2 * width) for b in (near, far)]).reshape(-1, 2 * width)
    other = swap(own)
    act = jnp.concatenate([act[:, :hidden], swap(act[:, hidden:])], axis=0)
    grad_hidden = jnp.concatenate([grad_hidden[:, :hidden], swap(grad_hidden[:, hidden:])], axis=0)
    x_all = jnp.concatenate([own[:, :width], other[:, :width]], axis=0)
    dy_all = jnp.concatenate([own[:, width:], other[:, width:]], axis=0)
    factor = 1.0 / math.sqrt(x_all.shape[0])
    grad_w_in = dot(x_all, grad_hidden, (0, 0))
    grad_w_out = dot(act, dy_all, (0, 0))
    return (
        grad_in.astype(bf16),
        (grad_w_in * factor).astype(bf16),
        (grad_w_out * factor).astype(bf16),
    )


def solution(mesh):
    rows, cols, deps = mesh.devices.shape
    fine = Mesh(
        mesh.devices.reshape(2, rows // 2, cols // 4, 2, 2, 2, deps // 4, 2),
        ("y_lo", "x", "y_far", "y_near", "core", "z_hi", "z_mid", "z_lo"),
    )
    blocks = ("y_far", "y_near", "core", "z_hi", "z_mid", "z_lo")
    placed = (P(blocks, ROWS), P(blocks, ROWS), P(ROWS, blocks), P(blocks, ROWS))
    return jax.shard_map(
        shards,
        mesh=fine,
        in_specs=placed,
        out_specs=(P(blocks, ROWS), P(ROWS, blocks), P(blocks, ROWS)),
        check_vma=False,
    )
```

```python
import functools
import math

import jax
import jax.numpy as jnp
from jax import lax
from jax.experimental import pallas as pl
from jax.experimental.pallas import tpu as pltpu
from jax.sharding import Mesh, PartitionSpec as P

coef = 0.7978845608
ROWS = ("y_lo", "x")
EVEN = ("y_far", "y_near", "z_hi", "z_mid")
CHIPS = ("y_far", "y_near", "z_hi", "z_lo", "z_mid")
RING = ("z_hi", "z_mid", "z_lo")


def gelu_value(h):
    u = coef * (h + 0.044715 * h * h * h)
    return 0.5 * h * (1.0 + jnp.tanh(u))


def gelu_slope(h):
    t = jnp.tanh(coef * (h + 0.044715 * h * h * h))
    return 0.5 * (1.0 + t) + 0.5 * h * (1.0 - t * t) * coef * (1.0 + 0.134145 * h * h)


def dot(a, b, dims):
    return lax.dot_general(a, b, ((dims[:1], dims[1:]), ((), ())), preferred_element_type=jnp.float32)


def exchange(blocks, axes):
    return lax.all_to_all(blocks, axes, 0, 0, tiled=True)


def spread(block, axes):
    n = lax.axis_size(axes)
    return exchange(jnp.broadcast_to(block[None], (n,) + block.shape), axes)


def swap(block):
    return lax.ppermute(block, "core", [(0, 1), (1, 0)])


def fetch(block, by):
    n = lax.axis_size(RING)
    return lax.ppermute(block, RING, [((i + by) % n, i) for i in range(n)])


def gather(block):
    near = spread(block, EVEN).reshape(-1, block.shape[1])
    cut = near.shape[0] // 2
    return near, [fetch(near[:cut], 1), fetch(near[cut:], -1)]


VMEM = pl.BlockSpec(memory_space=pltpu.VMEM)
HBM = pl.BlockSpec(memory_space=pltpu.HBM)
PARAMS = pltpu.CompilerParams(vmem_limit_bytes=16 * 2**20)


def in_hbm(*arrays):
    return [pltpu.with_memory_space_constraint(a, pltpu.HBM) for a in arrays]


def start_all(places, arrived):
    copies = [pltpu.make_async_copy(a, b, arrived.at[i]) for i, (a, b) in enumerate(places)]
    for copy in copies:
        copy.start()
    return copies


def hold_kernel(w_in, w_out, held_in, held_out, arrived):
    for copy in start_all([(w_in, held_in), (w_out, held_out)], arrived):
        copy.wait()


def hold(w_in, w_out):
    return pl.pallas_call(
        hold_kernel,
        out_shape=(pltpu.VMEM(w_in.shape, w_in.dtype), pltpu.VMEM(w_out.shape, w_out.dtype)),
        in_specs=[HBM, HBM],
        out_specs=(VMEM, VMEM),
        scratch_shapes=[pltpu.SemaphoreType.DMA((2,))],
        compiler_params=PARAMS,
        cost_estimate=pl.CostEstimate(flops=0, bytes_accessed=8 * w_in.size, transcendentals=0),
    )(*in_hbm(w_in, w_out))


def products_kernel(count, *refs):
    blocks = refs[:count]
    w_in, w_out, w_in_other, w_out_other, part, block, in_held, out_held, total, arrived, sent = refs[count:]
    width, hidden = w_in.shape
    rows = blocks[0].shape[0]
    copies = start_all(
        [(b, block.at[pl.ds(i * rows, rows)]) for i, b in enumerate(blocks)]
        + [(w_in_other, in_held), (w_out_other, out_held)],
        arrived,
    )
    for copy in copies[:count]:
        copy.wait()
    results = []
    for i, weight in enumerate((w_in, w_out, in_held, out_held)):
        if i >= 2:
            copies[count + i - 2].wait()
        if i % 2 == 0:
            value = dot(block[:, :width], weight[...], (1, 0))
        else:
            value = dot(block[:, width:], weight[...], (1, 1))
        place = pl.ds((i // 2 + 2 * (i % 2)) * hidden, hidden)
        total[:, place] = value.astype(total.dtype)
        results.append(pltpu.make_async_copy(total.at[:, place], part.at[:, place], sent.at[i]))
        results[i].start()
    for result in results:
        result.wait()


def products(blocks, held, others, weight):
    rows, (width, hidden) = sum(b.shape[0] for b in blocks), held[0].shape
    dtype, count = blocks[0].dtype, len(blocks)
    return pl.pallas_call(
        functools.partial(products_kernel, count),
        out_shape=jax.ShapeDtypeStruct((rows, 4 * hidden), dtype),
        in_specs=[HBM] * count + [VMEM] * 2 + [HBM] * 2,
        out_specs=HBM,
        scratch_shapes=[
            pltpu.VMEM((rows, 2 * width), dtype),
            pltpu.VMEM((width, hidden), dtype),
            pltpu.VMEM((hidden, width), dtype),
            pltpu.VMEM((rows, 4 * hidden), dtype),
            pltpu.SemaphoreType.DMA((count + 2,)),
            pltpu.SemaphoreType.DMA((4,)),
        ],
        compiler_params=PARAMS,
        cost_estimate=pl.CostEstimate(
            flops=8 * weight * rows * width * hidden, bytes_accessed=8 * width * hidden, transcendentals=0
        ),
    )(*in_hbm(*blocks), *held, *in_hbm(*others))


def input_kernel(pair, w_mine, w_other, out, grad_hidden, mine, other, total, arrived, sent):
    hidden = mine.shape[1]
    half = pair.shape[0] // 2
    copies = start_all(
        [(pair.at[:, 2 * hidden :], grad_hidden), (w_mine, mine), (w_other, other)], arrived
    )
    copies[0].wait()
    copies[1].wait()
    value = dot(grad_hidden[:, :hidden], mine[...], (1, 1))
    copies[2].wait()
    results = []
    for i in range(2):
        rows = pl.ds(i * half, half)
        part = value[i * half : (i + 1) * half] + dot(grad_hidden[rows, hidden:], other[...], (1, 1))
        total[rows, :] = part.astype(total.dtype)
        results.append(pltpu.make_async_copy(total.at[rows], out.at[rows], sent.at[i]))
        results[i].start()
    for result in results:
        result.wait()


def input_products(pair, w_in):
    rows, (width, hidden) = pair.shape[0], w_in[0].shape
    return pl.pallas_call(
        input_kernel,
        out_shape=jax.ShapeDtypeStruct((rows, width), pair.dtype),
        in_specs=[pl.BlockSpec(memory_space=pl.ANY)] + [HBM] * 2,
        out_specs=HBM,
        scratch_shapes=[
            pltpu.VMEM((rows, 2 * hidden), pair.dtype),
            pltpu.VMEM((width, hidden), pair.dtype),
            pltpu.VMEM((width, hidden), pair.dtype),
            pltpu.VMEM((rows, width), pair.dtype),
            pltpu.SemaphoreType.DMA((3,)),
            pltpu.SemaphoreType.DMA((2,)),
        ],
        compiler_params=PARAMS,
        cost_estimate=pl.CostEstimate(
            flops=4 * rows * width * hidden, bytes_accessed=6 * width * hidden, transcendentals=0
        ),
    )(pair, *in_hbm(*w_in))


def shards(tokens, grad_out, w_in, w_out):
    bf16, f32 = jnp.bfloat16, jnp.float32
    width, hidden = w_in.shape
    rows = lax.axis_size(ROWS)

    low = lax.axis_index("z_lo") == 0

    def by_z(near, far):
        return jnp.concatenate([jnp.where(low, near, far), jnp.where(low, far, near)], axis=-2)

    near, far = gather(jnp.concatenate([tokens, grad_out], axis=1))
    held, others = hold(w_in, w_out), [swap(w_in), swap(w_out)]
    parts = products([near], held, others, 25), products(far, held, others, 25)
    parts = [exchange(part.reshape(rows, -1, 4 * hidden), ROWS) for part in parts]
    total = by_z(*[jnp.sum(part.astype(f32), axis=0) for part in parts])
    pre, back = total[:, : 2 * hidden], total[:, 2 * hidden :]
    pair = jnp.concatenate([gelu_value(pre).astype(bf16), (back * gelu_slope(pre)).astype(bf16)], axis=1)
    pair = spread(pair, ROWS).reshape(-1, 4 * hidden)
    input_part = exchange(input_products(pair, [w_in, others[0]]).reshape(lax.axis_size(CHIPS), -1, width), CHIPS)
    grad_in = jnp.sum(input_part.astype(f32), axis=0)

    act, grad_hidden = pair[:, : 2 * hidden], pair[:, 2 * hidden :]
    far = jnp.concatenate(far, axis=0)
    own = by_z(*[b.reshape(rows, -1, 2 * width) for b in (near, far)]).reshape(-1, 2 * width)
    other = swap(own)
    act = jnp.concatenate([act[:, :hidden], swap(act[:, hidden:])], axis=0)
    grad_hidden = jnp.concatenate([grad_hidden[:, :hidden], swap(grad_hidden[:, hidden:])], axis=0)
    x_all = jnp.concatenate([own[:, :width], other[:, :width]], axis=0)
    dy_all = jnp.concatenate([own[:, width:], other[:, width:]], axis=0)
    factor = 1.0 / math.sqrt(x_all.shape[0])
    grad_w_in = dot(x_all, grad_hidden, (0, 0))
    grad_w_out = dot(act, dy_all, (0, 0))
    return (
        grad_in.astype(bf16),
        (grad_w_in * factor).astype(bf16),
        (grad_w_out * factor).astype(bf16),
    )


def solution(mesh):
    rows, cols, deps = mesh.devices.shape
    fine = Mesh(
        mesh.devices.reshape(2, rows // 2, cols // 4, 2, 2, 2, deps // 4, 2),
        ("y_lo", "x", "y_far", "y_near", "core", "z_hi", "z_mid", "z_lo"),
    )
    blocks = ("y_far", "y_near", "core", "z_hi", "z_mid", "z_lo")
    placed = (P(blocks, ROWS), P(blocks, ROWS), P(ROWS, blocks), P(blocks, ROWS))
    return jax.shard_map(
        shards,
        mesh=fine,
        in_specs=placed,
        out_specs=(P(blocks, ROWS), P(ROWS, blocks), P(blocks, ROWS)),
        check_vma=False,
    )
```

```python
import functools
import math

import jax
import jax.numpy as jnp
from jax import lax
from jax.experimental import pallas as pl
from jax.experimental.pallas import tpu as pltpu
from jax.sharding import Mesh, PartitionSpec as P

coef = 0.7978845608
ROWS = ("y_lo", "x")
EVEN = ("y_far", "y_near", "z_hi", "z_mid")
CHIPS = ("y_far", "y_near", "z_lo", "z_hi", "z_mid")
RING = ("z_hi", "z_mid", "z_lo")


def gelu_value(h):
    u = coef * (h + 0.044715 * h * h * h)
    return 0.5 * h * (1.0 + jnp.tanh(u))


def gelu_slope(h):
    t = jnp.tanh(coef * (h + 0.044715 * h * h * h))
    return 0.5 * (1.0 + t) + 0.5 * h * (1.0 - t * t) * coef * (1.0 + 0.134145 * h * h)


def dot(a, b, dims):
    return lax.dot_general(a, b, ((dims[:1], dims[1:]), ((), ())), preferred_element_type=jnp.float32)


def exchange(blocks, axes):
    return lax.all_to_all(blocks, axes, 0, 0, tiled=True)


def spread(block, axes):
    n = lax.axis_size(axes)
    return exchange(jnp.broadcast_to(block[None], (n,) + block.shape), axes)


def swap(block):
    return lax.ppermute(block, "core", [(0, 1), (1, 0)])


def fetch(block, by):
    n = lax.axis_size(RING)
    return lax.ppermute(block, RING, [((i + by) % n, i) for i in range(n)])


def gather(block):
    near = spread(block, EVEN).reshape(-1, block.shape[1])
    cut = near.shape[0] // 2
    return near, [fetch(near[:cut], 1), fetch(near[cut:], -1)]


VMEM = pl.BlockSpec(memory_space=pltpu.VMEM)
HBM = pl.BlockSpec(memory_space=pltpu.HBM)
PARAMS = pltpu.CompilerParams(vmem_limit_bytes=16 * 2**20)


def in_hbm(*arrays):
    return [pltpu.with_memory_space_constraint(a, pltpu.HBM) for a in arrays]


def start_all(places, arrived):
    copies = [pltpu.make_async_copy(a, b, arrived.at[i]) for i, (a, b) in enumerate(places)]
    for copy in copies:
        copy.start()
    return copies


def hold_kernel(w_in, w_out, held_in, held_out, arrived):
    for copy in start_all([(w_in, held_in), (w_out, held_out)], arrived):
        copy.wait()


def hold(w_in, w_out):
    return pl.pallas_call(
        hold_kernel,
        out_shape=(pltpu.VMEM(w_in.shape, w_in.dtype), pltpu.VMEM(w_out.shape, w_out.dtype)),
        in_specs=[HBM, HBM],
        out_specs=(VMEM, VMEM),
        scratch_shapes=[pltpu.SemaphoreType.DMA((2,))],
        compiler_params=PARAMS,
        cost_estimate=pl.CostEstimate(flops=0, bytes_accessed=8 * w_in.size, transcendentals=0),
    )(*in_hbm(w_in, w_out))


def products_kernel(count, *refs):
    blocks = refs[:count]
    w_in, w_out, w_in_other, w_out_other, part, block, in_held, out_held, total, arrived, sent = refs[count:]
    width, hidden = w_in.shape
    rows = blocks[0].shape[0]
    copies = start_all(
        [(b, block.at[pl.ds(i * rows, rows)]) for i, b in enumerate(blocks)]
        + [(w_in_other, in_held), (w_out_other, out_held)],
        arrived,
    )
    for copy in copies[:count]:
        copy.wait()
    results = []
    for i, weight in enumerate((w_in, w_out, in_held, out_held)):
        if i >= 2:
            copies[count + i - 2].wait()
        if i % 2 == 0:
            value = dot(block[:, :width], weight[...], (1, 0))
        else:
            value = dot(block[:, width:], weight[...], (1, 1))
        place = pl.ds((i // 2 + 2 * (i % 2)) * hidden, hidden)
        total[:, place] = value.astype(total.dtype)
        results.append(pltpu.make_async_copy(total.at[:, place], part.at[:, place], sent.at[i]))
        results[i].start()
    for result in results:
        result.wait()


def products(blocks, held, others, weight):
    rows, (width, hidden) = sum(b.shape[0] for b in blocks), held[0].shape
    dtype, count = blocks[0].dtype, len(blocks)
    return pl.pallas_call(
        functools.partial(products_kernel, count),
        out_shape=jax.ShapeDtypeStruct((rows, 4 * hidden), dtype),
        in_specs=[HBM] * count + [VMEM] * 2 + [HBM] * 2,
        out_specs=HBM,
        scratch_shapes=[
            pltpu.VMEM((rows, 2 * width), dtype),
            pltpu.VMEM((width, hidden), dtype),
            pltpu.VMEM((hidden, width), dtype),
            pltpu.VMEM((rows, 4 * hidden), dtype),
            pltpu.SemaphoreType.DMA((count + 2,)),
            pltpu.SemaphoreType.DMA((4,)),
        ],
        compiler_params=PARAMS,
        cost_estimate=pl.CostEstimate(
            flops=8 * weight * rows * width * hidden, bytes_accessed=8 * width * hidden, transcendentals=0
        ),
    )(*in_hbm(*blocks), *held, *in_hbm(*others))


def input_kernel(pair, w_mine, w_other, out, grad_hidden, mine, other, total, arrived, sent):
    width, hidden = mine.shape
    cut = width // 3
    pieces = [pl.ds(i * cut, cut) for i in range(3)]
    places = [(pair.at[:, 2 * hidden :], grad_hidden)]
    for piece in pieces:
        places += [(w_mine.at[piece], mine.at[piece]), (w_other.at[piece], other.at[piece])]
    copies = start_all(places, arrived)
    copies[0].wait()
    for i, piece in enumerate(pieces):
        copies[1 + 2 * i].wait()
        value = dot(grad_hidden[:, :hidden], mine[piece, :], (1, 1))
        copies[2 + 2 * i].wait()
        value = value + dot(grad_hidden[:, hidden:], other[piece, :], (1, 1))
        total[..., piece] = value.astype(total.dtype).reshape(total.shape[:-1] + (cut,))
    for result in start_all([(total.at[:, i, j], out.at[:, j, i]) for i in range(2) for j in range(2)], sent):
        result.wait()


def input_products(pair, w_in):
    rows, (width, hidden) = pair.shape[0], w_in[0].shape
    return pl.pallas_call(
        input_kernel,
        out_shape=jax.ShapeDtypeStruct((4, 2, 2, rows // 16, width), pair.dtype),
        in_specs=[pl.BlockSpec(memory_space=pl.ANY)] + [HBM] * 2,
        out_specs=HBM,
        scratch_shapes=[
            pltpu.VMEM((rows, 2 * hidden), pair.dtype),
            pltpu.VMEM((width, hidden), pair.dtype),
            pltpu.VMEM((width, hidden), pair.dtype),
            pltpu.VMEM((4, 2, 2, rows // 16, width), pair.dtype),
            pltpu.SemaphoreType.DMA((7,)),
            pltpu.SemaphoreType.DMA((4,)),
        ],
        compiler_params=PARAMS,
        cost_estimate=pl.CostEstimate(
            flops=4 * rows * width * hidden, bytes_accessed=6 * width * hidden, transcendentals=0
        ),
    )(pair, *in_hbm(*w_in))


def shards(tokens, grad_out, w_in, w_out):
    bf16, f32 = jnp.bfloat16, jnp.float32
    width, hidden = w_in.shape
    rows = lax.axis_size(ROWS)

    low = lax.axis_index("z_lo") == 0

    def by_z(near, far):
        return jnp.concatenate([jnp.where(low, near, far), jnp.where(low, far, near)], axis=-2)

    near, far = gather(jnp.concatenate([tokens, grad_out], axis=1))
    held, others = hold(w_in, w_out), [swap(w_in), swap(w_out)]
    parts = products([near], held, others, 25), products(far, held, others, 25)
    parts = [exchange(part.reshape(rows, -1, 4 * hidden), ROWS) for part in parts]
    total = by_z(*[jnp.sum(part.astype(f32), axis=0) for part in parts])
    pre, back = total[:, : 2 * hidden], total[:, 2 * hidden :]
    pair = jnp.concatenate([gelu_value(pre).astype(bf16), (back * gelu_slope(pre)).astype(bf16)], axis=1)
    pair = spread(pair, ROWS).reshape(-1, 4 * hidden)
    input_part = exchange(input_products(pair, [w_in, others[0]]).reshape(lax.axis_size(CHIPS), -1, width), CHIPS)
    grad_in = jnp.sum(input_part.astype(f32), axis=0)

    act, grad_hidden = pair[:, : 2 * hidden], pair[:, 2 * hidden :]
    far = jnp.concatenate(far, axis=0)
    own = by_z(*[b.reshape(rows, -1, 2 * width) for b in (near, far)]).reshape(-1, 2 * width)
    other = swap(own)
    act = jnp.concatenate([act[:, :hidden], swap(act[:, hidden:])], axis=0)
    grad_hidden = jnp.concatenate([grad_hidden[:, :hidden], swap(grad_hidden[:, hidden:])], axis=0)
    x_all = jnp.concatenate([own[:, :width], other[:, :width]], axis=0)
    dy_all = jnp.concatenate([own[:, width:], other[:, width:]], axis=0)
    factor = 1.0 / math.sqrt(x_all.shape[0])
    grad_w_in = dot(x_all, grad_hidden, (0, 0))
    grad_w_out = dot(act, dy_all, (0, 0))
    return (
        grad_in.astype(bf16),
        (grad_w_in * factor).astype(bf16),
        (grad_w_out * factor).astype(bf16),
    )


def solution(mesh):
    rows, cols, deps = mesh.devices.shape
    fine = Mesh(
        mesh.devices.reshape(2, rows // 2, cols // 4, 2, 2, 2, deps // 4, 2),
        ("y_lo", "x", "y_far", "y_near", "core", "z_hi", "z_mid", "z_lo"),
    )
    blocks = ("y_far", "y_near", "core", "z_hi", "z_mid", "z_lo")
    placed = (P(blocks, ROWS), P(blocks, ROWS), P(ROWS, blocks), P(blocks, ROWS))
    return jax.shard_map(
        shards,
        mesh=fine,
        in_specs=placed,
        out_specs=(P(blocks, ROWS), P(ROWS, blocks), P(blocks, ROWS)),
        check_vma=False,
    )
```
